256 devices in a mesh: grp: 2 (over core), row: 4 (over x), col: 32 (over z, y).
Axes of the slice: x: 4, y: 4, z: 8, core: 2. Of those that a mesh axis runs over, the one named last changes fastest.
Arguments:
- front_matrix: float32 [2, 8192, 8192], P('grp', 'row', 'col'), may hold values from -1 to 41
- row_pattern: int32 [2, 64], replicated, may hold values from 0 to 1, as said below
- col_pattern: int32 [2, 64], replicated, may hold values from 0 to 1, as said below
Outputs:
- contribution: float32 [8192, 8192], P('row', 'col')
The draws below stay inside these ranges and needn't reach their ends.
Inputs may be any that keep to these rules, and one draw needn't show every extreme that they name: `row_pattern`: entries are 0 or 1; entries 0 and 1 of each row are 1. `col_pattern`: entries are 0 or 1; entries 0 and 1 of each row are 1.
All inputs are finite; a program needn't handle non-finite values.
Results may differ from the reference program's by a relative error of at most 0.0001.
Values sent between devices are 32-bit elements; how exact they have to be, the bound alone decides.
A program may use at most 64 MiB of HBM per device.

```python
import jax
import jax.numpy as jnp
from jax import lax

B = 128
STEPS = 2
GRPS = 2
NB = 64
N = 8192


def draw_front_matrix(key, part):
    values = jax.random.uniform(key, (GRPS, N, N), jnp.float32, -1.0, 1.0)
    rows_at = jnp.arange(N, dtype=jnp.int32)[:, None]
    cols_at = jnp.arange(N, dtype=jnp.int32)[None, :]
    boost = jnp.where((rows_at == cols_at) & (rows_at < STEPS * B), 40.0, 0.0)
    return values + boost[None, :, :]


def draw_row_pattern(key, part):
    marks = jax.random.randint(jax.random.fold_in(key, 11), (STEPS, NB), 0, 2)
    return jnp.where(jnp.arange(NB, dtype=jnp.int32)[None, :] < 2, 1, marks).astype(jnp.int32)


def draw_col_pattern(key, part):
    marks = jax.random.randint(jax.random.fold_in(key, 23), (STEPS, NB), 0, 2)
    return jnp.where(jnp.arange(NB, dtype=jnp.int32)[None, :] < 2, 1, marks).astype(jnp.int32)


def setup_inputs(seed: int = 0) -> dict:
    key_list = jax.random.split(jax.random.key(seed), 4)
    return {
        "front_matrix": draw_front_matrix(jax.random.fold_in(key_list[3], 71), 0),
        "row_pattern": draw_row_pattern(jax.random.fold_in(key_list[3], 71), 0),
        "col_pattern": draw_col_pattern(jax.random.fold_in(key_list[3], 71), 0),
    }


def factor_block(block):
    extent = block.shape[0]
    places = jnp.arange(extent, dtype=jnp.int32)

    def sweep(k, packed):
        pivot_value = packed[k, k]
        below_col = jnp.where(places > k, packed[:, k] / pivot_value, 0.0)
        right_row = jnp.where(places > k, packed[k, :], 0.0)
        packed = packed - below_col[:, None] * right_row[None, :]
        packed = jnp.where((places[None, :] == k) & (places[:, None] > k), below_col[:, None], packed)
        return packed
    packed = lax.fori_loop(0, extent, sweep, block)
    lower_unit = jnp.tril(packed, -1) + jnp.eye(extent, dtype=packed.dtype)
    upper_tri = jnp.triu(packed)
    return (lower_unit, upper_tri)

def reference(front_matrix, row_pattern, col_pattern):
    highest = lax.Precision.HIGHEST
    blocks = jnp.arange(N, dtype=jnp.int32) // B
    contribution = jnp.zeros((N, N), jnp.float32)
    for group in range(GRPS):
        working = front_matrix[group]
        for k in range(STEPS):
            keep_rows = jnp.repeat(row_pattern[k], B)
            keep_cols = jnp.repeat(col_pattern[k], B)
            working = jnp.where((blocks == k)[None, :] & (keep_rows == 0)[:, None], 0.0, working)
            working = jnp.where((blocks == k)[:, None] & (keep_cols == 0)[None, :], 0.0, working)
        for k in range(STEPS):
            corner = working[k * B:(k + 1) * B, k * B:(k + 1) * B]
            lower_unit, upper_tri = factor_block(corner)
            lower_rows = jax.scipy.linalg.solve_triangular(upper_tri, working[:, k * B:(k + 1) * B].T, trans=1, lower=False).T
            lower_rows = jnp.where((blocks > k)[:, None], lower_rows, 0.0)
            upper_cols = jax.scipy.linalg.solve_triangular(lower_unit, working[k * B:(k + 1) * B, :], lower=True, unit_diagonal=True)
            upper_cols = jnp.where((blocks > k)[None, :], upper_cols, 0.0)
            working = working - jnp.dot(lower_rows, upper_cols, precision=highest)
        trailing = (blocks >= STEPS)[:, None] & (blocks >= STEPS)[None, :]
        contribution = contribution + jnp.where(trailing, working, 0.0)
    return contribution
```

```python
import jax
import jax.numpy as jnp
from jax import lax
from jax.experimental import pallas as pl
from jax.experimental.pallas import tpu as pltpu
from jax.sharding import PartitionSpec as P

B = 128
PIV = 256
ROWS = 2048
COLS = 256
NB = 16
NZ, NY, NX = 8, 4, 4
HALF = ROWS // 2
CHUNKS = 16
CROWS = HALF // CHUNKS
ICHUNKS = 4
IROWS = PIV // 2 // ICHUNKS
LAG = 7
TILE = 256
TILES = ROWS // TILE
MESH = pl.DeviceIdType.MESH


def split(x):
    high = x.astype(jnp.bfloat16)
    low = (x - high.astype(jnp.float32)).astype(jnp.bfloat16)
    return high, low


def dot3(a, b):
    f32 = jnp.float32
    total = jnp.dot(a[1], b[0], preferred_element_type=f32)
    total = total + jnp.dot(a[0], b[1], preferred_element_type=f32)
    return total + jnp.dot(a[0], b[0], preferred_element_type=f32)


def eliminate(rows, first):
    cols = [jnp.broadcast_to(rows[:, first + j : first + j + 1], (NB, B)) for j in range(NB)]
    place = lax.broadcasted_iota(jnp.int32, (NB, B), 0)
    for k in range(NB):
        here = place == k
        column = cols[k]
        recip = 1.0 / jnp.broadcast_to(column[k : k + 1, :], (NB, B))
        for j in range(NB):
            if j != k:
                scaled = jnp.broadcast_to(cols[j][k : k + 1, :], (NB, B)) * recip
                cols[j] = jnp.where(here, scaled, cols[j] - column * scaled)
        cols[k] = jnp.where(here, recip, -column * recip)
    lane = lax.broadcasted_iota(jnp.int32, (NB, PIV), 1)
    row = lax.broadcasted_iota(jnp.int32, (NB, PIV), 0)
    rows = jnp.where((lane >= first) & (lane < first + NB), jnp.where(lane == first + row, 1.0, 0.0), rows)
    total = None
    for j in range(NB):
        term = jnp.concatenate([cols[j]] * (PIV // B), axis=1) * jnp.broadcast_to(rows[j : j + 1, :], (NB, PIV))
        total = term if total is None else total + term
    return total


def invert(block, between):
    lane = lax.broadcasted_iota(jnp.int32, (PIV, PIV), 1)
    for step in range(PIV // NB):
        first = step * NB
        row_part = eliminate(block[first : first + NB, :], first)
        col_part = block[:, first : first + NB]
        rest = jnp.where((lane >= first) & (lane < first + NB), 0.0, block[...])
        block[...] = rest - jnp.dot(
            col_part, row_part, precision=lax.Precision.HIGHEST, preferred_element_type=jnp.float32
        )
        block[first : first + NB, :] = row_part
        between(step)


def kernel(
    front, row_pattern, col_pattern, out,
    panel, mine, above, inverse, peer, total,
    panel_recv, panel_send, inv_recv, inv_send, above_recv, above_send, peer_recv, peer_send,
    out_sem, load_sem,
):
    g = lax.axis_index("grp")
    r = lax.axis_index("row")
    c = lax.axis_index("col")
    z = c // NY
    y = c % NY

    def at(dx=0, dz=0, dy=0):
        zz = lax.rem(z + dz + NZ, NZ)
        yy = lax.rem(y + dy + NY, NY)
        return (g, lax.rem(r + dx + NX, NX), zz * NY + yy)

    other = (1 - g, r, c)
    near = [at(dz=1), at(dz=-1), at(dy=1), at(dy=-1)]
    beside = [at(dx=1), at(dx=2), at(dx=3)]
    targets = near + [at(dx=1), at(dx=-1)]

    barrier = pltpu.get_barrier_semaphore()
    for device in near + beside + [other]:
        pl.semaphore_signal(barrier, inc=1, device_id=device, device_id_type=MESH)

    root = c == 0
    owner = root & (r == 0)
    up = z <= 3
    down = (z == 0) | (z >= 6)
    flags = (
        (
            (y == 0) & up,
            ((y == 0) & down) | ((y != 0) & (z == 1)),
            (z != 0) & (y <= 1),
            (z != 0) & (y == 0),
            root & (r <= 1),
            root & (r == 0),
        ),
        (
            (y != 0) & up,
            (y != 0) & down,
            (z == 0) & (y <= 1),
            root | ((z != 0) & (y == 1)),
            root & (r == 0),
            root & ((r == 0) | (r == 3)),
        ),
    )
    late = (((z == 0) & (y != 0)).astype(jnp.int32), ((y == 0) & (z != 0)).astype(jnp.int32))

    load_mine = pltpu.make_async_copy(front.at[0], mine, load_sem.at[0])
    load_mine.start()
    load_pivot = pltpu.make_async_copy(front.at[0, 0:PIV, :], inverse, load_sem.at[1])
    load_above = pltpu.make_async_copy(front.at[0, 0:PIV, :], above, load_sem.at[2])
    load_panel = pltpu.make_async_copy(front.at[0], panel, load_sem.at[3])

    @pl.when(owner)
    def _():
        load_pivot.start()

    @pl.when(r == 0)
    def _():
        load_above.start()

    @pl.when(root)
    def _():
        load_panel.start()

    pl.semaphore_wait(barrier, len(near) + len(beside) + 1)

    def panel_rows(tree, chunk):
        return pl.ds(tree * HALF + chunk * CROWS, CROWS)

    def send_panel(source, tree, chunk, slot):
        rows = panel_rows(tree, chunk)
        pltpu.make_async_remote_copy(
            source.at[rows, :], panel.at[rows, :], panel_send.at[tree, slot], panel_recv.at[tree, chunk],
            device_id=targets[slot], device_id_type=MESH,
        ).start()

    def root_sends(chunk):
        send_panel(front.at[0], 0, chunk, 0)
        send_panel(front.at[0], 1, chunk, 2)
        send_panel(front.at[0], 0, chunk, 1)
        send_panel(front.at[0], 1, chunk, 3)

    def send_above(slot):
        return pltpu.make_async_remote_copy(
            front.at[0, 0:PIV, :], above, above_send.at[slot], above_recv,
            device_id=beside[slot], device_id_type=MESH,
        )

    @pl.when(r == 0)
    def _():
        for slot in range(3):
            send_above(slot).start()

    def inverse_rows(tree, chunk):
        return pl.ds(tree * (PIV // 2) + chunk * IROWS, IROWS)

    def inverse_copy(tree, chunk, slot):
        rows = inverse_rows(tree, chunk)
        return pltpu.make_async_remote_copy(
            inverse.at[rows, :], inverse.at[rows, :], inv_send.at[tree, slot], inv_recv.at[tree, chunk],
            device_id=targets[slot], device_id_type=MESH,
        )

    @pl.when(owner)
    def _():
        load_pivot.wait()

        def between(step):
            if step < CHUNKS // 2:
                root_sends(2 * step)
                root_sends(2 * step + 1)

        invert(inverse, between)
        for chunk in range(ICHUNKS):
            for slot in (4, 5, 0, 1, 2, 3):
                for tree in range(2):

                    @pl.when(flags[tree][slot])
                    def _(tree=tree, slot=slot, chunk=chunk):
                        inverse_copy(tree, chunk, slot).start()

    @pl.when(root & (r != 0))
    def _():
        def body(chunk, carry):
            root_sends(chunk)
            return carry

        lax.fori_loop(0, CHUNKS, body, 0)

    @pl.when(jnp.logical_not(root))
    def _():
        def body(step, carry):
            for tree in range(2):
                chunk = step - LAG * late[tree]

                @pl.when((chunk >= 0) & (chunk < CHUNKS))
                def _(tree=tree, chunk=chunk):
                    rows = panel_rows(tree, chunk)
                    pltpu.make_async_copy(panel.at[rows, :], panel.at[rows, :], panel_recv.at[tree, chunk]).wait()
                    for slot in range(4):

                        @pl.when(flags[tree][slot])
                        def _(slot=slot):
                            send_panel(panel, tree, chunk, slot)

            return carry

        lax.fori_loop(0, CHUNKS + LAG, body, 0)

    @pl.when(jnp.logical_not(owner))
    def _():
        def body(step, carry):
            for tree in range(2):
                chunk = step - ICHUNKS * late[tree]

                @pl.when((chunk >= 0) & (chunk < ICHUNKS))
                def _(tree=tree, chunk=chunk):
                    rows = inverse_rows(tree, chunk)
                    pltpu.make_async_copy(inverse.at[rows, :], inverse.at[rows, :], inv_recv.at[tree, chunk]).wait()
                    for slot in (4, 5, 0, 1, 2, 3):

                        @pl.when(flags[tree][slot])
                        def _(slot=slot):
                            inverse_copy(tree, chunk, slot).start()

            return carry

        lax.fori_loop(0, 2 * ICHUNKS, body, 0)

    load_mine.wait()

    @pl.when(r == 0)
    def _():
        load_above.wait()

    @pl.when(r != 0)
    def _():
        send_above(0).wait_recv()

    @pl.when(root)
    def _():
        load_panel.wait()

    place = lax.broadcasted_iota(jnp.int32, (PIV, COLS), 0)
    across = lax.broadcasted_iota(jnp.int32, (PIV, COLS), 1)
    keep = jnp.where(
        place < B,
        jnp.where(across < B, col_pattern[0, 2 * c], col_pattern[0, 2 * c + 1]),
        jnp.where(across < B, col_pattern[1, 2 * c], col_pattern[1, 2 * c + 1]),
    )
    right = jnp.where(keep != 0, above[...], 0.0)
    solved = jnp.dot(
        inverse[...], right, precision=lax.Precision.HIGHEST, preferred_element_type=jnp.float32
    )
    solved = split(solved)

    def exchange(tile):
        rows = pl.ds(tile * TILE, TILE)
        return pltpu.make_async_remote_copy(
            mine.at[rows, :], peer.at[rows, :], peer_send, peer_recv.at[tile],
            device_id=other, device_id_type=MESH,
        )

    def store_out(tile):
        rows = pl.ds(tile * TILE, TILE)
        return pltpu.make_async_copy(total.at[rows, :], out.at[rows, :], out_sem)

    for tile in range(TILES + 2):
        if tile < TILES:
            rows = slice(tile * TILE, (tile + 1) * TILE)
            i = r * (ROWS // B) + 2 * tile
            keep = jnp.where(
                place < B,
                jnp.where(across < B, row_pattern[0, i], row_pattern[1, i]),
                jnp.where(across < B, row_pattern[0, i + 1], row_pattern[1, i + 1]),
            )
            left = split(jnp.where(keep != 0, panel[rows, :], 0.0))
            update = mine[rows, :] - dot3(left, solved)
            trailing = jnp.logical_not(root) & (i >= 2)
            mine[rows, :] = jnp.where(trailing, update, 0.0)
            exchange(tile).start()
        if tile >= 2:
            done = tile - 2
            rows = slice(done * TILE, (done + 1) * TILE)
            exchange(done).wait_recv()
            total[rows, :] = mine[rows, :] + peer[rows, :]
            store_out(done).start()

    pltpu.make_async_copy(total, out, out_sem).wait()
    pltpu.make_async_copy(mine, mine, peer_send).wait()

    @pl.when(r == 0)
    def _():
        for slot in range(3):
            send_above(slot).wait_send()

    for tree in range(2):
        half = pl.ds(tree * HALF, HALF)
        part = pl.ds(tree * (PIV // 2), PIV // 2)
        for slot in range(6):

            @pl.when(flags[tree][slot])
            def _(tree=tree, slot=slot, half=half, part=part):
                if slot < 4:
                    pltpu.make_async_copy(panel.at[half, :], panel.at[half, :], panel_send.at[tree, slot]).wait()
                pltpu.make_async_copy(inverse.at[part, :], inverse.at[part, :], inv_send.at[tree, slot]).wait()


def shards(front_matrix, row_pattern, col_pattern):
    f32 = jnp.float32
    dma = pltpu.SemaphoreType.DMA
    return pl.pallas_call(
        kernel,
        out_shape=jax.ShapeDtypeStruct((ROWS, COLS), f32),
        in_specs=[
            pl.BlockSpec(memory_space=pl.ANY),
            pl.BlockSpec(memory_space=pltpu.SMEM),
            pl.BlockSpec(memory_space=pltpu.SMEM),
        ],
        out_specs=pl.BlockSpec(memory_space=pl.ANY),
        scratch_shapes=[
            pltpu.VMEM((ROWS, COLS), f32),
            pltpu.VMEM((ROWS, COLS), f32),
            pltpu.VMEM((PIV, COLS), f32),
            pltpu.VMEM((PIV, PIV), f32),
            pltpu.VMEM((ROWS, COLS), f32),
            pltpu.VMEM((ROWS, COLS), f32),
            dma((2, CHUNKS)),
            dma((2, 4)),
            dma((2, ICHUNKS)),
            dma((2, 6)),
            dma(()),
            dma((3,)),
            dma((TILES,)),
            dma(()),
            dma(()),
            dma((4,)),
        ],
        compiler_params=pltpu.CompilerParams(
            collective_id=0, has_side_effects=True, vmem_limit_bytes=32 * 1024 * 1024
        ),
        cost_estimate=pl.CostEstimate(
            flops=2 * ROWS * COLS * PIV, bytes_accessed=6 * ROWS * COLS * 4, transcendentals=0
        ),
        name="panel_update",
    )(front_matrix, row_pattern, col_pattern)


def solution(mesh):
    in_specs = (P("grp", "row", "col"), P(), P())
    out_specs = P("row", "col")
    return jax.shard_map(shards, mesh=mesh, in_specs=in_specs, out_specs=out_specs, check_vma=False)
```

```python
import jax
import jax.numpy as jnp
from jax import lax
from jax.experimental import pallas as pl
from jax.experimental.pallas import tpu as pltpu
from jax.sharding import PartitionSpec as P

B = 128
PIV = 256
ROWS = 2048
COLS = 256
NB = 16
NZ, NY, NX = 8, 4, 4
TREES = 4
QUARTER = ROWS // TREES
CROWS = 16
CHUNKS = QUARTER // CROWS
IQUARTER = PIV // TREES
ICHUNKS = IQUARTER // CROWS
PLACES = CHUNKS + ICHUNKS
SPAN = PLACES * CROWS
AHEAD = CHUNKS * 3 // 4
LEVEL = 80
TILE = 256
TILES = ROWS // TILE
LATER = 3
MESH = pl.DeviceIdType.MESH

STEPS_IN = (
    (0, 1, 2, 3), (1, 0, 2, 3), (1, 0, 2, 3), (1, 0, 2, 3),
    (0, 1, 3, 2), (2, 3, 0, 1), (2, 0, 1, 3), (1, 2, 3, 0),
    (0, 1, 3, 2), (2, 1, 0, 3), (1, 0, 2, 3), (3, 1, 2, 0),
    (0, 1, 3, 2), (2, 1, 0, 3), (3, 1, 2, 0), (3, 1, 2, 0),
    (0, 1, 3, 2), (2, 1, 0, 3), (3, 2, 0, 1), (3, 1, 2, 0),
    (0, 1, 3, 2), (0, 2, 1, 3), (0, 2, 1, 3), (0, 3, 2, 1),
    (0, 1, 3, 2), (0, 2, 1, 3), (1, 0, 2, 3), (0, 3, 2, 1),
    (0, 1, 3, 2), (3, 2, 1, 0), (1, 2, 0, 3), (2, 0, 3, 1),
)


def walk(chip, direction, back=False):
    z, y = divmod(chip, NY)
    move = -1 if back else 1
    dz, dy = ((1, 0), (-1, 0), (0, 1), (0, -1))[direction]
    return (z + move * dz) % NZ * NY + (y + move * dy) % NY


def bits(values):
    word = sum(1 << chip for chip, value in enumerate(values) if value)
    return word - (1 << 32) if word >= 1 << 31 else word


def depth(tree, chip):
    steps = 0
    while chip:
        chip = walk(chip, STEPS_IN[chip][tree], back=True)
        steps += 1
    return steps


PLANE = range(NZ * NY)
DEPTHS = [[depth(tree, chip) for chip in PLANE] for tree in range(TREES)]


def carried(chip, direction):
    child = walk(chip, direction)
    return STEPS_IN[child].index(direction) if child else None


CARRIED = [[carried(n, d) for n in PLANE] for d in range(4)]
OUT = [bits([CARRIED[d][n] is not None for n in PLANE]) for d in range(4)]
TREE_BITS = [[bits([(CARRIED[d][n] or 0) >> b & 1 for n in PLANE]) for b in range(2)] for d in range(4)]
FIRST = [
    bits([CARRIED[d][n] is not None and CARRIED[d][n] not in [CARRIED[e][n] for e in range(d)] for n in PLANE])
    for d in range(4)
]
LEAF = [bits([all(CARRIED[d][n] != t for d in range(4)) for n in PLANE]) for t in range(TREES)]


def behind(chip, direction):
    trees = [CARRIED[d][chip] for d in range(4) if CARRIED[d][chip] is not None]
    mine = CARRIED[direction][chip]
    return 0 if mine is None else DEPTHS[mine][chip] - min(DEPTHS[t][chip] for t in trees)


BEHIND = [[behind(n, d) for n in PLANE] for d in range(4)]
BEHIND_BITS = [[bits([v >> b & 1 for v in BEHIND[d]]) for b in range(3)] for d in range(4)]
LONGEST = max(max(line) for line in BEHIND) * LEVEL // 10
ROOT_WAY = [next(d for d in range(4) if CARRIED[d][0] == t) for t in range(TREES)]


def split(x):
    high = x.astype(jnp.bfloat16)
    low = (x - high.astype(jnp.float32)).astype(jnp.bfloat16)
    return high, low


def stacked_dot(a, b):
    left = jnp.concatenate([a[0], a[0], a[1]], axis=1)
    right = jnp.concatenate([b[0], b[1], b[0]], axis=0)
    return jnp.dot(left, right, preferred_element_type=jnp.float32)


def along(column, width):
    return jnp.concatenate([column] * (width // B), axis=1)


def eliminate(rows, first):
    cols = [jnp.broadcast_to(rows[:, first + j : first + j + 1], (NB, B)) for j in range(NB)]
    place = lax.broadcasted_iota(jnp.int32, (NB, B), 0)
    for k in range(NB):
        here = place == k
        column = cols[k]
        recip = 1.0 / jnp.broadcast_to(column[k : k + 1, :], (NB, B))
        for j in range(NB):
            if j != k:
                scaled = jnp.broadcast_to(cols[j][k : k + 1, :], (NB, B)) * recip
                cols[j] = jnp.where(here, scaled, cols[j] - column * scaled)
        cols[k] = jnp.where(here, recip, -column * recip)
    lane = lax.broadcasted_iota(jnp.int32, (NB, PIV), 1)
    row = lax.broadcasted_iota(jnp.int32, (NB, PIV), 0)
    rows = jnp.where((lane >= first) & (lane < first + NB), jnp.where(lane == first + row, 1.0, 0.0), rows)
    return outer_sum(cols, rows)


def outer_sum(cols, rows):
    total = None
    for j in range(NB):
        term = along(cols[j], PIV) * jnp.broadcast_to(rows[j : j + 1, :], (NB, PIV))
        total = term if total is None else total + term
    return total


def invert(block, between):
    lane = lax.broadcasted_iota(jnp.int32, (PIV, PIV), 1)
    rows = block[0:NB, :]
    for step in range(PIV // NB):
        first = step * NB
        end = first + NB
        row_part = eliminate(rows, first)
        if end < PIV:
            rows = block[end : end + NB, :]
            cols = [jnp.broadcast_to(rows[:, first + j : first + j + 1], (NB, B)) for j in range(NB)]
            rows = jnp.where((lane[:NB] >= first) & (lane[:NB] < end), 0.0, rows) - outer_sum(cols, row_part)
        rest = jnp.where((lane >= first) & (lane < end), 0.0, block[...])
        block[...] = rest - stacked_dot(split(block[:, first:end]), split(row_part))
        block[first:end, :] = row_part
        if end < PIV:
            block[end : end + NB, :] = rows
        between(step)


def kernel(
    front, row_table, col_table, out,
    stream, mine, above, inverse, peer, total, row_pattern, col_pattern,
    recv_sem, send_sem, cross_sem, above_recv, above_send, peer_recv, peer_send, out_sem, load_sem,
):
    g = lax.axis_index("grp")
    r = lax.axis_index("row")
    c = lax.axis_index("col")
    z = c // NY
    y = c % NY

    def at(dx=0, dz=0, dy=0):
        zz = lax.rem(z + dz + NZ, NZ)
        yy = lax.rem(y + dy + NY, NY)
        return (g, lax.rem(r + dx + NX, NX), zz * NY + yy)

    def bit(word):
        return lax.shift_right_logical(jnp.int32(word), c) & 1

    def number(words):
        return sum(bit(word) << place for place, word in enumerate(words))

    other = (1 - g, r, c)
    near = [at(dz=1), at(dz=-1), at(dy=1), at(dy=-1)]
    beside = [at(dx=1), at(dx=2), at(dx=3)]

    barrier = pltpu.get_barrier_semaphore()
    for device in near + beside + [other]:
        pl.semaphore_signal(barrier, inc=1, device_id=device, device_id_type=MESH)

    first_plane = r == 0
    root = c == 0
    owner = root & first_plane
    worker = jnp.logical_not(root)
    out_tree = [number(TREE_BITS[d]) for d in range(4)]
    plus = [root & (first_plane | ((r == 1) if t < 2 else False)) for t in range(TREES)]
    minus = [root & (first_plane | ((r == 3) if t >= 2 else False)) for t in range(TREES)]
    ahead = jnp.where(first_plane, AHEAD, CHUNKS)

    load_pivot = pltpu.make_async_copy(front.at[0, 0:PIV, :], inverse, load_sem.at[1])
    load_mine = pltpu.make_async_copy(front.at[0], mine, load_sem.at[0])
    load_above = pltpu.make_async_copy(front.at[0, 0:PIV, :], above, load_sem.at[2])
    load_rows = pltpu.make_async_copy(row_table, row_pattern, load_sem.at[3])
    load_cols = pltpu.make_async_copy(col_table, col_pattern, load_sem.at[4])

    @pl.when(owner)
    def _():
        load_pivot.start()

    @pl.when(worker)
    def _():
        load_rows.start()
        load_cols.start()
        load_mine.start()

    @pl.when(worker & first_plane)
    def _():
        load_above.start()

    pl.semaphore_wait(barrier, len(near) + len(beside) + 1)

    def places(tree, place):
        return pl.ds(pl.multiple_of(tree * SPAN + place * CROWS, CROWS), CROWS)

    def pass_on(source, tree, place, way):
        pltpu.make_async_remote_copy(
            source, stream.at[places(tree, place), :], send_sem.at[way], recv_sem.at[tree, place],
            device_id=near[way], device_id_type=MESH,
        ).start()

    def take(tree, place):
        rows = places(tree, place)
        pltpu.make_async_copy(stream.at[rows, :], stream.at[rows, :], recv_sem.at[tree, place]).wait()

    def cross(source, tree, chunk, way):
        pltpu.make_async_remote_copy(
            source, stream.at[places(tree, CHUNKS + chunk), :], cross_sem.at[tree, way],
            recv_sem.at[tree, CHUNKS + chunk],
            device_id=(beside[0], beside[2])[way], device_id_type=MESH,
        ).start()

    def root_sends(chunk, place):
        for tree in range(TREES):
            rows = pl.ds(pl.multiple_of(tree * QUARTER + chunk * CROWS, CROWS), CROWS)
            pass_on(front.at[0, rows, :], tree, place, ROOT_WAY[tree])

    def send_above(slot):
        return pltpu.make_async_remote_copy(
            front.at[0, 0:PIV, :], above, above_send.at[slot], above_recv,
            device_id=beside[slot], device_id_type=MESH,
        )

    @pl.when(worker & first_plane)
    def _():
        for slot in range(3):
            send_above(slot).start()

    @pl.when(owner)
    def _():
        load_pivot.wait()
        steps = PIV // NB

        def between(step):
            for chunk in range(step * AHEAD // steps, (step + 1) * AHEAD // steps):
                root_sends(chunk, chunk)

        invert(inverse, between)
        for chunk in range(ICHUNKS):
            for tree in range(TREES):
                source = inverse.at[pl.ds(tree * IQUARTER + chunk * CROWS, CROWS), :]
                cross(source, tree, chunk, 0)
                cross(source, tree, chunk, 1)
                pass_on(source, tree, AHEAD + chunk, ROOT_WAY[tree])
        for chunk in range(AHEAD, CHUNKS):
            root_sends(chunk, chunk + ICHUNKS)

    @pl.when(root & (r != 0))
    def _():
        def body(chunk, carry):
            root_sends(chunk, chunk)
            return carry

        lax.fori_loop(0, CHUNKS, body, 0)
        for chunk in range(ICHUNKS):
            for tree in range(TREES):
                source = stream.at[places(tree, CHUNKS + chunk), :]
                take(tree, CHUNKS + chunk)

                @pl.when(plus[tree])
                def _(source=source, tree=tree, chunk=chunk):
                    cross(source, tree, chunk, 0)

                @pl.when(minus[tree])
                def _(source=source, tree=tree, chunk=chunk):
                    cross(source, tree, chunk, 1)

                pass_on(source, tree, CHUNKS + chunk, ROOT_WAY[tree])

    @pl.when(worker)
    def _():
        leaf = [bit(LEAF[t]) == 1 for t in range(TREES)]
        first = [bit(FIRST[d]) == 1 for d in range(4)]
        starts = [(number(BEHIND_BITS[d]) * LEVEL) // 10 for d in range(4)]
        lengths = [bit(OUT[d]) * PLACES for d in range(4)]

        def body(step, carry):
            for way in range(4):
                place = step - starts[way]

                @pl.when((place >= 0) & (place < lengths[way]))
                def _(way=way, place=place):
                    tree = out_tree[way]

                    @pl.when(first[way])
                    def _():
                        take(tree, place)

                    pass_on(stream.at[places(tree, place), :], tree, place, way)

            return carry

        lax.fori_loop(0, PLACES + LONGEST, body, 0)

        for tree in range(TREES):

            @pl.when(leaf[tree])
            def _(tree=tree):
                def rest(place, carry):
                    take(tree, place)
                    return carry

                lax.fori_loop(0, PLACES, rest, 0)

        load_mine.wait()
        load_rows.wait()
        load_cols.wait()

        @pl.when(first_plane)
        def _():
            load_above.wait()

        @pl.when(r != 0)
        def _():
            send_above(0).wait_recv()

        place = lax.broadcasted_iota(jnp.int32, (PIV, COLS), 0)
        across = lax.broadcasted_iota(jnp.int32, (PIV, COLS), 1)
        keep = jnp.where(
            place < B,
            jnp.where(across < B, col_pattern[0, 2 * c], col_pattern[0, 2 * c + 1]),
            jnp.where(across < B, col_pattern[1, 2 * c], col_pattern[1, 2 * c + 1]),
        )
        right = split(jnp.where(keep != 0, above[...], 0.0))
        solve = jnp.concatenate(
            [
                stream[pl.ds(pl.multiple_of(tree * SPAN + ahead * CROWS, CROWS), IQUARTER), :]
                for tree in range(TREES)
            ],
            axis=0,
        )
        solved = split(stacked_dot(split(solve), right))
        stack = jnp.concatenate([solved[0], solved[1], solved[0]], axis=0)

        def block_row(index):
            chunk = index * B // CROWS % CHUNKS
            start = index * B // QUARTER * SPAN + chunk * CROWS
            if chunk >= AHEAD:
                start = start + jnp.where(first_plane, ICHUNKS * CROWS, 0)
            block = stream[pl.ds(pl.multiple_of(start, CROWS), B), :]
            i = r * (ROWS // B) + index
            keep = jnp.where(across[:B] < B, row_pattern[0, i], row_pattern[1, i])
            return split(jnp.where(keep != 0, block, 0.0))

        def exchange(tile):
            rows = pl.ds(tile * TILE, TILE)
            return pltpu.make_async_remote_copy(
                mine.at[rows, :], peer.at[rows, :], peer_send, peer_recv.at[tile],
                device_id=other, device_id_type=MESH,
            )

        def store_out(tile):
            rows = pl.ds(tile * TILE, TILE)
            return pltpu.make_async_copy(total.at[rows, :], out.at[rows, :], out_sem)

        for tile in range(TILES + LATER):
            if tile < TILES:
                rows = slice(tile * TILE, (tile + 1) * TILE)
                parts = [block_row(tile * (TILE // B) + b) for b in range(TILE // B)]
                high = jnp.concatenate([part[0] for part in parts], axis=0)
                low = jnp.concatenate([part[1] for part in parts], axis=0)
                left = jnp.concatenate([high, high, low], axis=1)
                update = mine[rows, :] - jnp.dot(left, stack, preferred_element_type=jnp.float32)
                if tile == 0:
                    update = jnp.where(r != 0, update, 0.0)
                mine[rows, :] = update
                exchange(tile).start()
            if tile >= LATER:
                done = tile - LATER
                rows = slice(done * TILE, (done + 1) * TILE)
                exchange(done).wait_recv()
                total[rows, :] = mine[rows, :] + peer[rows, :]
                store_out(done).start()

        pltpu.make_async_copy(total, out, out_sem).wait()
        pltpu.make_async_copy(mine, mine, peer_send).wait()

        @pl.when(first_plane)
        def _():
            for slot in range(3):
                send_above(slot).wait_send()

    @pl.when(root)
    def _():
        total[...] = jnp.zeros_like(total)
        clear = pltpu.make_async_copy(total, out, out_sem)
        clear.start()
        clear.wait()

    def sent(rows, semaphore):
        pltpu.make_async_copy(stream.at[0:rows, :], stream.at[0:rows, :], semaphore).wait()

    for way in range(4):

        @pl.when(bit(OUT[way]) == 1)
        def _(way=way):
            sent(SPAN, send_sem.at[way])

    for tree in range(TREES):
        for way, crossed in enumerate((plus[tree], minus[tree])):

            @pl.when(crossed)
            def _(tree=tree, way=way):
                sent(IQUARTER, cross_sem.at[tree, way])


def shards(front_matrix, row_pattern, col_pattern):
    f32, i32 = jnp.float32, jnp.int32
    dma = pltpu.SemaphoreType.DMA
    return pl.pallas_call(
        kernel,
        out_shape=jax.ShapeDtypeStruct((ROWS, COLS), f32),
        in_specs=[pl.BlockSpec(memory_space=pltpu.HBM)] * 3,
        out_specs=pl.BlockSpec(memory_space=pl.ANY),
        scratch_shapes=[
            pltpu.VMEM((TREES * SPAN, COLS), f32),
            pltpu.VMEM((ROWS, COLS), f32),
            pltpu.VMEM((PIV, COLS), f32),
            pltpu.VMEM((PIV, PIV), f32),
            pltpu.VMEM((ROWS, COLS), f32),
            pltpu.VMEM((ROWS, COLS), f32),
            pltpu.SMEM((2, 64), i32),
            pltpu.SMEM((2, 64), i32),
            dma((TREES, PLACES)),
            dma((4,)),
            dma((TREES, 2)),
            dma(()),
            dma((3,)),
            dma((TILES,)),
            dma(()),
            dma(()),
            dma((5,)),
        ],
        compiler_params=pltpu.CompilerParams(
            collective_id=0, has_side_effects=True, vmem_limit_bytes=50 * 1024 * 1024
        ),
        cost_estimate=pl.CostEstimate(
            flops=2 * ROWS * COLS * PIV, bytes_accessed=6 * ROWS * COLS * 4, transcendentals=0
        ),
        name="panel_update",
    )(front_matrix, row_pattern, col_pattern)


def solution(mesh):
    in_specs = (P("grp", "row", "col"), P(), P())
    out_specs = P("row", "col")
    return jax.shard_map(shards, mesh=mesh, in_specs=in_specs, out_specs=out_specs, check_vma=False)
```

```python
import jax
import jax.numpy as jnp
from jax import lax
from jax.experimental import pallas as pl
from jax.experimental.pallas import tpu as pltpu
from jax.sharding import PartitionSpec as P

B = 128
PIV = 256
ROWS = 2048
COLS = 256
NB = 16
NZ, NY, NX = 8, 4, 4
TREES = 4
QUARTER = ROWS // TREES
CROWS = 16
CHUNKS = QUARTER // CROWS
IQUARTER = PIV // TREES
ICHUNKS = IQUARTER // CROWS
PLACES = CHUNKS + ICHUNKS
SPAN = PLACES * CROWS
AHEAD = CHUNKS * 3 // 4
LEVEL = 100
TILE = 256
TILES = ROWS // TILE
LATER = 3
MESH = pl.DeviceIdType.MESH

STEPS_IN = (
    (0, 1, 2, 3), (1, 0, 2, 3), (1, 0, 2, 3), (1, 0, 2, 3),
    (0, 1, 3, 2), (2, 3, 0, 1), (2, 0, 1, 3), (1, 2, 3, 0),
    (0, 1, 3, 2), (2, 1, 0, 3), (1, 0, 2, 3), (3, 1, 2, 0),
    (0, 1, 3, 2), (2, 1, 0, 3), (3, 1, 2, 0), (3, 1, 2, 0),
    (0, 1, 3, 2), (2, 1, 0, 3), (3, 2, 0, 1), (3, 1, 2, 0),
    (0, 1, 3, 2), (0, 2, 1, 3), (0, 2, 1, 3), (0, 3, 2, 1),
    (0, 1, 3, 2), (0, 2, 1, 3), (1, 0, 2, 3), (0, 3, 2, 1),
    (0, 1, 3, 2), (3, 2, 1, 0), (1, 2, 0, 3), (2, 0, 3, 1),
)


def walk(chip, direction, back=False):
    z, y = divmod(chip, NY)
    move = -1 if back else 1
    dz, dy = ((1, 0), (-1, 0), (0, 1), (0, -1))[direction]
    return (z + move * dz) % NZ * NY + (y + move * dy) % NY


def bits(values):
    word = sum(1 << chip for chip, value in enumerate(values) if value)
    return word - (1 << 32) if word >= 1 << 31 else word


def depth(tree, chip):
    steps = 0
    while chip:
        chip = walk(chip, STEPS_IN[chip][tree], back=True)
        steps += 1
    return steps


PLANE = range(NZ * NY)
DEPTHS = [[depth(tree, chip) for chip in PLANE] for tree in range(TREES)]


def carried(chip, direction):
    child = walk(chip, direction)
    return STEPS_IN[child].index(direction) if child else None


CARRIED = [[carried(n, d) for n in PLANE] for d in range(4)]
OUT = [bits([CARRIED[d][n] is not None for n in PLANE]) for d in range(4)]
TREE_BITS = [[bits([(CARRIED[d][n] or 0) >> b & 1 for n in PLANE]) for b in range(2)] for d in range(4)]
FIRST = [
    bits([CARRIED[d][n] is not None and CARRIED[d][n] not in [CARRIED[e][n] for e in range(d)] for n in PLANE])
    for d in range(4)
]
LEAF = [bits([all(CARRIED[d][n] != t for d in range(4)) for n in PLANE]) for t in range(TREES)]


def behind(chip, direction):
    trees = [CARRIED[d][chip] for d in range(4) if CARRIED[d][chip] is not None]
    mine = CARRIED[direction][chip]
    return 0 if mine is None else DEPTHS[mine][chip] - min(DEPTHS[t][chip] for t in trees)


BEHIND = [[behind(n, d) for n in PLANE] for d in range(4)]
BEHIND_BITS = [[bits([v >> b & 1 for v in BEHIND[d]]) for b in range(3)] for d in range(4)]
LONGEST = max(max(line) for line in BEHIND) * LEVEL // 10
ROOT_WAY = [next(d for d in range(4) if CARRIED[d][0] == t) for t in range(TREES)]


INWARD = [(base + step % 2, step // 2) for base in (0, 2) for step in range(2 * ICHUNKS)]


def split(x):
    high = x.astype(jnp.bfloat16)
    low = (x - high.astype(jnp.float32)).astype(jnp.bfloat16)
    return high, low


def stacked_dot(a, b):
    left = jnp.concatenate([a[0], a[0], a[1]], axis=1)
    right = jnp.concatenate([b[0], b[1], b[0]], axis=0)
    return jnp.dot(left, right, preferred_element_type=jnp.float32)


def along(column, width):
    return jnp.concatenate([column] * (width // B), axis=1)


def eliminate(rows, first):
    cols = [jnp.broadcast_to(rows[:, first + j : first + j + 1], (NB, B)) for j in range(NB)]
    place = lax.broadcasted_iota(jnp.int32, (NB, B), 0)
    for k in range(NB):
        here = place == k
        column = cols[k]
        recip = 1.0 / jnp.broadcast_to(column[k : k + 1, :], (NB, B))
        for j in range(NB):
            if j != k:
                scaled = jnp.broadcast_to(cols[j][k : k + 1, :], (NB, B)) * recip
                cols[j] = jnp.where(here, scaled, cols[j] - column * scaled)
        cols[k] = jnp.where(here, recip, -column * recip)
    lane = lax.broadcasted_iota(jnp.int32, (NB, PIV), 1)
    row = lax.broadcasted_iota(jnp.int32, (NB, PIV), 0)
    rows = jnp.where((lane >= first) & (lane < first + NB), jnp.where(lane == first + row, 1.0, 0.0), rows)
    return outer_sum(cols, rows)


def outer_sum(cols, rows):
    total = None
    for j in range(NB):
        term = along(cols[j], PIV) * jnp.broadcast_to(rows[j : j + 1, :], (NB, PIV))
        total = term if total is None else total + term
    return total


def invert(block, between):
    lane = lax.broadcasted_iota(jnp.int32, (PIV, PIV), 1)
    rows = block[0:NB, :]
    for step in range(PIV // NB):
        first = step * NB
        end = first + NB
        row_part = eliminate(rows, first)
        if end < PIV:
            rows = block[end : end + NB, :]
            cols = [jnp.broadcast_to(rows[:, first + j : first + j + 1], (NB, B)) for j in range(NB)]
            rows = jnp.where((lane[:NB] >= first) & (lane[:NB] < end), 0.0, rows) - outer_sum(cols, row_part)
        rest = jnp.where((lane >= first) & (lane < end), 0.0, block[...])
        block[...] = rest - stacked_dot(split(block[:, first:end]), split(row_part))
        block[first:end, :] = row_part
        if end < PIV:
            block[end : end + NB, :] = rows
        between(step)


def kernel(
    front, table, out,
    stream, mine, above, inverse, peer, total, patterns,
    recv_sem, send_sem, cross_sem, above_recv, above_send, peer_recv, peer_send, out_sem, load_sem,
):
    g = lax.axis_index("grp")
    r = lax.axis_index("row")
    c = lax.axis_index("col")
    z = c // NY
    y = c % NY

    def at(dx=0, dz=0, dy=0):
        zz = lax.rem(z + dz + NZ, NZ)
        yy = lax.rem(y + dy + NY, NY)
        return (g, lax.rem(r + dx + NX, NX), zz * NY + yy)

    def bit(word):
        return lax.shift_right_logical(jnp.int32(word), c) & 1

    def number(words):
        return sum(bit(word) << place for place, word in enumerate(words))

    other = (1 - g, r, c)
    near = [at(dz=1), at(dz=-1), at(dy=1), at(dy=-1)]
    beside = [at(dx=1), at(dx=2), at(dx=3)]

    barrier = pltpu.get_barrier_semaphore()
    for device in near + beside + [other]:
        pl.semaphore_signal(barrier, inc=1, device_id=device, device_id_type=MESH)

    first_plane = r == 0
    root = c == 0
    owner = root & first_plane
    worker = jnp.logical_not(root)
    out_tree = [number(TREE_BITS[d]) for d in range(4)]
    plus = [root & (first_plane | ((r == 1) if t < 2 else False)) for t in range(TREES)]
    minus = [root & (first_plane | ((r == 3) if t >= 2 else False)) for t in range(TREES)]
    ahead = jnp.where(first_plane, AHEAD, CHUNKS)

    load_pivot = pltpu.make_async_copy(front.at[0, 0:PIV, :], inverse, load_sem.at[1])
    load_mine = pltpu.make_async_copy(front.at[0], mine, load_sem.at[0])
    load_above = pltpu.make_async_copy(front.at[0, 0:PIV, :], above, load_sem.at[2])
    load_table = pltpu.make_async_copy(table, patterns, load_sem.at[3])

    @pl.when(owner)
    def _():
        load_pivot.start()

    @pl.when(worker)
    def _():
        load_table.start()
        load_mine.start()

    @pl.when(worker & first_plane)
    def _():
        load_above.start()

    pl.semaphore_wait(barrier, len(near) + len(beside) + 1)

    def places(tree, place):
        return pl.ds(pl.multiple_of(tree * SPAN + place * CROWS, CROWS), CROWS)

    def pass_on(source, tree, place, way):
        pltpu.make_async_remote_copy(
            source, stream.at[places(tree, place), :], send_sem.at[way], recv_sem.at[tree, place],
            device_id=near[way], device_id_type=MESH,
        ).start()

    def take(tree, place):
        rows = places(tree, place)
        pltpu.make_async_copy(stream.at[rows, :], stream.at[rows, :], recv_sem.at[tree, place]).wait()

    def cross(source, tree, chunk, way):
        pltpu.make_async_remote_copy(
            source, stream.at[places(tree, CHUNKS + chunk), :], cross_sem.at[tree, way],
            recv_sem.at[tree, CHUNKS + chunk],
            device_id=(beside[0], beside[2])[way], device_id_type=MESH,
        ).start()

    def root_sends(chunk, place):
        for tree in range(TREES):
            rows = pl.ds(pl.multiple_of(tree * QUARTER + chunk * CROWS, CROWS), CROWS)
            pass_on(front.at[0, rows, :], tree, place, ROOT_WAY[tree])

    def send_above(slot):
        return pltpu.make_async_remote_copy(
            front.at[0, 0:PIV, :], above, above_send.at[slot], above_recv,
            device_id=beside[slot], device_id_type=MESH,
        )

    @pl.when(worker & first_plane)
    def _():
        for slot in range(3):
            send_above(slot).start()

    @pl.when(owner)
    def _():
        load_pivot.wait()
        steps = PIV // NB

        def between(step):
            for chunk in range(step * AHEAD // steps, (step + 1) * AHEAD // steps):
                root_sends(chunk, chunk)

        invert(inverse, between)

        def quarter(tree, chunk):
            return inverse.at[pl.ds(tree * IQUARTER + chunk * CROWS, CROWS), :]

        for step in range(TREES * ICHUNKS):
            tree, chunk = INWARD[step]
            cross(quarter(tree, chunk), tree, chunk, 0)
            tree = (tree + 2) % TREES
            cross(quarter(tree, chunk), tree, chunk, 1)
            tree, chunk = step % TREES, step // TREES
            pass_on(quarter(tree, chunk), tree, AHEAD + chunk, ROOT_WAY[tree])
        for chunk in range(AHEAD, CHUNKS):
            root_sends(chunk, chunk + ICHUNKS)

    @pl.when(root & (r != 0))
    def _():
        def body(chunk, carry):
            root_sends(chunk, chunk)
            return carry

        lax.fori_loop(0, CHUNKS, body, 0)

        for plane in (1, 2, 3):

            @pl.when(r == plane)
            def _(plane=plane):
                for step in range(TREES * ICHUNKS):
                    tree, chunk = INWARD[step]
                    if plane == 2:
                        tree, chunk = (0, 2, 1, 3)[step % TREES], step // TREES
                    if plane == 3:
                        tree = (tree + 2) % TREES
                    source = stream.at[places(tree, CHUNKS + chunk), :]
                    take(tree, CHUNKS + chunk)
                    if plane == 1 and tree < 2:
                        cross(source, tree, chunk, 0)
                    if plane == 3 and tree >= 2:
                        cross(source, tree, chunk, 1)
                    pass_on(source, tree, CHUNKS + chunk, ROOT_WAY[tree])

    @pl.when(worker)
    def _():
        leaf = [bit(LEAF[t]) == 1 for t in range(TREES)]
        first = [bit(FIRST[d]) == 1 for d in range(4)]
        starts = [(number(BEHIND_BITS[d]) * LEVEL) // 10 for d in range(4)]
        lengths = [bit(OUT[d]) * PLACES for d in range(4)]

        def body(step, carry):
            for way in range(4):
                place = step - starts[way]

                @pl.when((place >= 0) & (place < lengths[way]))
                def _(way=way, place=place):
                    tree = out_tree[way]

                    @pl.when(first[way])
                    def _():
                        take(tree, place)

                    pass_on(stream.at[places(tree, place), :], tree, place, way)

            return carry

        lax.fori_loop(0, PLACES + LONGEST, body, 0)

        for tree in range(TREES):

            @pl.when(leaf[tree])
            def _(tree=tree):
                def rest(place, carry):
                    take(tree, place)
                    return carry

                lax.fori_loop(0, PLACES, rest, 0)

        load_mine.wait()
        load_table.wait()

        @pl.when(first_plane)
        def _():
            load_above.wait()

        @pl.when(r != 0)
        def _():
            send_above(0).wait_recv()

        place = lax.broadcasted_iota(jnp.int32, (PIV, COLS), 0)
        across = lax.broadcasted_iota(jnp.int32, (PIV, COLS), 1)
        keep = jnp.where(
            place < B,
            jnp.where(across < B, patterns[2, 2 * c], patterns[2, 2 * c + 1]),
            jnp.where(across < B, patterns[3, 2 * c], patterns[3, 2 * c + 1]),
        )
        right = split(jnp.where(keep != 0, above[...], 0.0))
        solve = jnp.concatenate(
            [
                stream[pl.ds(pl.multiple_of(tree * SPAN + ahead * CROWS, CROWS), IQUARTER), :]
                for tree in range(TREES)
            ],
            axis=0,
        )
        solved = split(stacked_dot(split(solve), right))
        stack = jnp.concatenate([solved[0], solved[1], solved[0]], axis=0)

        def block_row(index):
            chunk = index * B // CROWS % CHUNKS
            start = index * B // QUARTER * SPAN + chunk * CROWS
            if chunk >= AHEAD:
                start = start + jnp.where(first_plane, ICHUNKS * CROWS, 0)
            block = stream[pl.ds(pl.multiple_of(start, CROWS), B), :]
            i = r * (ROWS // B) + index
            keep = jnp.where(across[:B] < B, patterns[0, i], patterns[1, i])
            return split(jnp.where(keep != 0, block, 0.0))

        def exchange(tile):
            rows = pl.ds(tile * TILE, TILE)
            return pltpu.make_async_remote_copy(
                mine.at[rows, :], peer.at[rows, :], peer_send, peer_recv.at[tile],
                device_id=other, device_id_type=MESH,
            )

        def store_out(tile):
            rows = pl.ds(tile * TILE, TILE)
            return pltpu.make_async_copy(total.at[rows, :], out.at[rows, :], out_sem)

        for tile in range(TILES + LATER):
            if tile < TILES:
                rows = slice(tile * TILE, (tile + 1) * TILE)
                parts = [block_row(tile * (TILE // B) + b) for b in range(TILE // B)]
                high = jnp.concatenate([part[0] for part in parts], axis=0)
                low = jnp.concatenate([part[1] for part in parts], axis=0)
                left = jnp.concatenate([high, high, low], axis=1)
                update = mine[rows, :] - jnp.dot(left, stack, preferred_element_type=jnp.float32)
                if tile * TILE < PIV:
                    update = jnp.where(r != 0, update, 0.0)
                mine[rows, :] = update
                exchange(tile).start()
            if tile >= LATER:
                done = tile - LATER
                rows = slice(done * TILE, (done + 1) * TILE)
                exchange(done).wait_recv()
                total[rows, :] = mine[rows, :] + peer[rows, :]
                store_out(done).start()

        pltpu.make_async_copy(total, out, out_sem).wait()
        pltpu.make_async_copy(mine, mine, peer_send).wait()

        @pl.when(first_plane)
        def _():
            for slot in range(3):
                send_above(slot).wait_send()

    @pl.when(root)
    def _():
        total[...] = jnp.zeros_like(total)
        clear = pltpu.make_async_copy(total, out, out_sem)
        clear.start()
        clear.wait()

    def sent(rows, semaphore):
        pltpu.make_async_copy(stream.at[0:rows, :], stream.at[0:rows, :], semaphore).wait()

    for way in range(4):

        @pl.when(bit(OUT[way]) == 1)
        def _(way=way):
            sent(SPAN, send_sem.at[way])

    for tree in range(TREES):
        for way, crossed in enumerate((plus[tree], minus[tree])):

            @pl.when(crossed)
            def _(tree=tree, way=way):
                sent(IQUARTER, cross_sem.at[tree, way])


def shards(front_matrix, row_pattern, col_pattern):
    f32, i32 = jnp.float32, jnp.int32
    dma = pltpu.SemaphoreType.DMA
    return pl.pallas_call(
        kernel,
        out_shape=jax.ShapeDtypeStruct((ROWS, COLS), f32),
        in_specs=[pl.BlockSpec(memory_space=pltpu.HBM)] * 2,
        out_specs=pl.BlockSpec(memory_space=pl.ANY),
        scratch_shapes=[
            pltpu.VMEM((TREES * SPAN, COLS), f32),
            pltpu.VMEM((ROWS, COLS), f32),
            pltpu.VMEM((PIV, COLS), f32),
            pltpu.VMEM((PIV, PIV), f32),
            pltpu.VMEM((ROWS, COLS), f32),
            pltpu.VMEM((ROWS, COLS), f32),
            pltpu.SMEM((4, 64), i32),
            dma((TREES, PLACES)),
            dma((4,)),
            dma((TREES, 2)),
            dma(()),
            dma((3,)),
            dma((TILES,)),
            dma(()),
            dma(()),
            dma((4,)),
        ],
        compiler_params=pltpu.CompilerParams(
            collective_id=0, has_side_effects=True, vmem_limit_bytes=50 * 1024 * 1024
        ),
        cost_estimate=pl.CostEstimate(
            flops=2 * ROWS * COLS * PIV, bytes_accessed=6 * ROWS * COLS * 4, transcendentals=0
        ),
        name="panel_update",
    )(front_matrix, jnp.concatenate([row_pattern, col_pattern]))


def solution(mesh):
    in_specs = (P("grp", "row", "col"), P(), P())
    out_specs = P("row", "col")
    return jax.shard_map(shards, mesh=mesh, in_specs=in_specs, out_specs=out_specs, check_vma=False)
```

```python
import jax
import jax.numpy as jnp
from jax import lax
from jax.experimental import pallas as pl
from jax.experimental.pallas import tpu as pltpu
from jax.sharding import PartitionSpec as P

B = 128
PIV = 256
ROWS = 2048
COLS = 256
NB = 16
NZ, NY, NX = 8, 4, 4
TREES = 4
QUARTER = ROWS // TREES
CROWS = 16
CHUNKS = QUARTER // CROWS
IQUARTER = PIV // TREES
ICHUNKS = IQUARTER // CROWS
PLACES = CHUNKS + ICHUNKS
SPAN = PLACES * CROWS
AHEAD = CHUNKS * 3 // 4
LEVEL = 100
TILE = 256
TILES = ROWS // TILE
LATER = 5
MESH = pl.DeviceIdType.MESH

STEPS_IN = (
    (0, 1, 2, 3), (1, 0, 2, 3), (1, 0, 2, 3), (1, 0, 2, 3),
    (0, 1, 3, 2), (2, 3, 0, 1), (2, 0, 1, 3), (1, 2, 3, 0),
    (0, 1, 3, 2), (2, 1, 0, 3), (1, 0, 2, 3), (3, 1, 2, 0),
    (0, 1, 3, 2), (2, 1, 0, 3), (3, 1, 2, 0), (3, 1, 2, 0),
    (0, 1, 3, 2), (2, 1, 0, 3), (3, 2, 0, 1), (3, 1, 2, 0),
    (0, 1, 3, 2), (0, 2, 1, 3), (0, 2, 1, 3), (0, 3, 2, 1),
    (0, 1, 3, 2), (0, 2, 1, 3), (1, 0, 2, 3), (0, 3, 2, 1),
    (0, 1, 3, 2), (3, 2, 1, 0), (1, 2, 0, 3), (2, 0, 3, 1),
)


def walk(chip, direction, back=False):
    z, y = divmod(chip, NY)
    move = -1 if back else 1
    dz, dy = ((1, 0), (-1, 0), (0, 1), (0, -1))[direction]
    return (z + move * dz) % NZ * NY + (y + move * dy) % NY


def bits(values):
    word = sum(1 << chip for chip, value in enumerate(values) if value)
    return word - (1 << 32) if word >= 1 << 31 else word


def depth(tree, chip):
    steps = 0
    while chip:
        chip = walk(chip, STEPS_IN[chip][tree], back=True)
        steps += 1
    return steps


PLANE = range(NZ * NY)
DEPTHS = [[depth(tree, chip) for chip in PLANE] for tree in range(TREES)]


def carried(chip, direction):
    child = walk(chip, direction)
    return STEPS_IN[child].index(direction) if child else None


CARRIED = [[carried(n, d) for n in PLANE] for d in range(4)]
OUT = [bits([CARRIED[d][n] is not None for n in PLANE]) for d in range(4)]
TREE_BITS = [[bits([(CARRIED[d][n] or 0) >> b & 1 for n in PLANE]) for b in range(2)] for d in range(4)]
FIRST = [
    bits([CARRIED[d][n] is not None and CARRIED[d][n] not in [CARRIED[e][n] for e in range(d)] for n in PLANE])
    for d in range(4)
]
LEAF = [bits([all(CARRIED[d][n] != t for d in range(4)) for n in PLANE]) for t in range(TREES)]


def behind(chip, direction):
    trees = [CARRIED[d][chip] for d in range(4) if CARRIED[d][chip] is not None]
    mine = CARRIED[direction][chip]
    return 0 if mine is None else DEPTHS[mine][chip] - min(DEPTHS[t][chip] for t in trees)


BEHIND = [[behind(n, d) for n in PLANE] for d in range(4)]
BEHIND_BITS = [[bits([v >> b & 1 for v in BEHIND[d]]) for b in range(3)] for d in range(4)]
LONGEST = max(max(line) for line in BEHIND) * LEVEL // 10
ROOT_WAY = [next(d for d in range(4) if CARRIED[d][0] == t) for t in range(TREES)]


INWARD = [(base + step % 2, step // 2) for base in (0, 2) for step in range(2 * ICHUNKS)]


def split(x):
    high = x.astype(jnp.bfloat16)
    low = (x - high.astype(jnp.float32)).astype(jnp.bfloat16)
    return high, low


def stacked_dot(a, b):
    left = jnp.concatenate([a[0], a[0], a[1]], axis=1)
    right = jnp.concatenate([b[0], b[1], b[0]], axis=0)
    return jnp.dot(left, right, preferred_element_type=jnp.float32)


def along(column, width):
    return jnp.concatenate([column] * (width // B), axis=1)


def eliminate(rows, first):
    cols = [jnp.broadcast_to(rows[:, first + j : first + j + 1], (NB, B)) for j in range(NB)]
    place = lax.broadcasted_iota(jnp.int32, (NB, B), 0)
    for k in range(NB):
        here = place == k
        column = cols[k]
        recip = pl.reciprocal(jnp.broadcast_to(column[k : k + 1, :], (NB, B)))
        for j in range(NB):
            if j != k:
                scaled = jnp.broadcast_to(cols[j][k : k + 1, :], (NB, B)) * recip
                cols[j] = jnp.where(here, scaled, cols[j] - column * scaled)
        cols[k] = jnp.where(here, recip, -column * recip)
    lane = lax.broadcasted_iota(jnp.int32, (NB, PIV), 1)
    row = lax.broadcasted_iota(jnp.int32, (NB, PIV), 0)
    rows = jnp.where((lane >= first) & (lane < first + NB), jnp.where(lane == first + row, 1.0, 0.0), rows)
    return outer_sum(cols, rows)


def outer_sum(cols, rows):
    total = None
    for j in range(NB):
        term = along(cols[j], PIV) * jnp.broadcast_to(rows[j : j + 1, :], (NB, PIV))
        total = term if total is None else total + term
    return total


def invert(block, between):
    lane = lax.broadcasted_iota(jnp.int32, (PIV, PIV), 1)
    rows = block[0:NB, :]
    for step in range(PIV // NB):
        first = step * NB
        end = first + NB
        row_part = eliminate(rows, first)
        if end < PIV:
            rows = block[end : end + NB, :]
            cols = [jnp.broadcast_to(rows[:, first + j : first + j + 1], (NB, B)) for j in range(NB)]
            rows = jnp.where((lane[:NB] >= first) & (lane[:NB] < end), 0.0, rows) - outer_sum(cols, row_part)
        rest = jnp.where((lane >= first) & (lane < end), 0.0, block[...])
        block[...] = rest - stacked_dot(split(block[:, first:end]), split(row_part))
        block[first:end, :] = row_part
        if end < PIV:
            block[end : end + NB, :] = rows
        between(step)


def kernel(
    front, table, out,
    stream, mine, above, inverse, peer, total, patterns,
    recv_sem, send_sem, cross_sem, above_recv, above_send, peer_recv, peer_send, out_sem, load_sem,
):
    g = lax.axis_index("grp")
    r = lax.axis_index("row")
    c = lax.axis_index("col")
    z = c // NY
    y = c % NY

    def at(dx=0, dz=0, dy=0):
        zz = lax.rem(z + dz + NZ, NZ)
        yy = lax.rem(y + dy + NY, NY)
        return (g, lax.rem(r + dx + NX, NX), zz * NY + yy)

    def bit(word):
        return lax.shift_right_logical(jnp.int32(word), c) & 1

    def number(words):
        return sum(bit(word) << place for place, word in enumerate(words))

    other = (1 - g, r, c)
    near = [at(dz=1), at(dz=-1), at(dy=1), at(dy=-1)]
    beside = [at(dx=1), at(dx=2), at(dx=3)]

    barrier = pltpu.get_barrier_semaphore()
    for device in near + beside + [other]:
        pl.semaphore_signal(barrier, inc=1, device_id=device, device_id_type=MESH)

    first_plane = r == 0
    root = c == 0
    owner = root & first_plane
    worker = jnp.logical_not(root)
    out_tree = [number(TREE_BITS[d]) for d in range(4)]
    plus = [root & (first_plane | ((r == 1) if t < 2 else False)) for t in range(TREES)]
    minus = [root & (first_plane | ((r == 3) if t >= 2 else False)) for t in range(TREES)]
    ahead = jnp.where(first_plane, AHEAD, CHUNKS)

    load_pivot = pltpu.make_async_copy(front.at[0, 0:PIV, :], inverse, load_sem.at[1])
    load_mine = pltpu.make_async_copy(front.at[0], mine, load_sem.at[0])
    load_above = pltpu.make_async_copy(front.at[0, 0:PIV, :], above, load_sem.at[2])
    load_table = pltpu.make_async_copy(table, patterns, load_sem.at[3])

    @pl.when(owner)
    def _():
        load_pivot.start()

    @pl.when(worker)
    def _():
        load_table.start()
        load_mine.start()

    @pl.when(worker & first_plane)
    def _():
        load_above.start()

    pl.semaphore_wait(barrier, len(near) + len(beside) + 1)

    def places(tree, place):
        return pl.ds(pl.multiple_of(tree * SPAN + place * CROWS, CROWS), CROWS)

    def pass_on(source, tree, place, way):
        pltpu.make_async_remote_copy(
            source, stream.at[places(tree, place), :], send_sem.at[way], recv_sem.at[tree, place],
            device_id=near[way], device_id_type=MESH,
        ).start()

    def take(tree, place):
        rows = places(tree, place)
        pltpu.make_async_copy(stream.at[rows, :], stream.at[rows, :], recv_sem.at[tree, place]).wait()

    def cross(source, tree, chunk, way):
        pltpu.make_async_remote_copy(
            source, stream.at[places(tree, CHUNKS + chunk), :], cross_sem.at[tree, way],
            recv_sem.at[tree, CHUNKS + chunk],
            device_id=(beside[0], beside[2])[way], device_id_type=MESH,
        ).start()

    def root_sends(chunk, place):
        for tree in range(TREES):
            rows = pl.ds(pl.multiple_of(tree * QUARTER + chunk * CROWS, CROWS), CROWS)
            pass_on(front.at[0, rows, :], tree, place, ROOT_WAY[tree])

    def send_above(slot):
        return pltpu.make_async_remote_copy(
            front.at[0, 0:PIV, :], above, above_send.at[slot], above_recv,
            device_id=beside[slot], device_id_type=MESH,
        )

    @pl.when(worker & first_plane)
    def _():
        for slot in range(3):
            send_above(slot).start()

    @pl.when(owner)
    def _():
        load_pivot.wait()
        steps = PIV // NB

        def between(step):
            for chunk in range(step * AHEAD // steps, (step + 1) * AHEAD // steps):
                root_sends(chunk, chunk)

        invert(inverse, between)

        def quarter(tree, chunk):
            return inverse.at[pl.ds(tree * IQUARTER + chunk * CROWS, CROWS), :]

        for step in range(TREES * ICHUNKS):
            tree, chunk = INWARD[step]
            cross(quarter(tree, chunk), tree, chunk, 0)
            tree = (tree + 2) % TREES
            cross(quarter(tree, chunk), tree, chunk, 1)
            tree, chunk = step % TREES, step // TREES
            pass_on(quarter(tree, chunk), tree, AHEAD + chunk, ROOT_WAY[tree])
        for chunk in range(AHEAD, CHUNKS):
            root_sends(chunk, chunk + ICHUNKS)

    @pl.when(root & (r != 0))
    def _():
        def body(chunk, carry):
            root_sends(chunk, chunk)
            return carry

        lax.fori_loop(0, CHUNKS, body, 0)

        for plane in (1, 2, 3):

            @pl.when(r == plane)
            def _(plane=plane):
                for step in range(TREES * ICHUNKS):
                    tree, chunk = INWARD[step]
                    if plane == 2:
                        tree, chunk = (0, 2, 1, 3)[step % TREES], step // TREES
                    if plane == 3:
                        tree = (tree + 2) % TREES
                    source = stream.at[places(tree, CHUNKS + chunk), :]
                    take(tree, CHUNKS + chunk)
                    if plane == 1 and tree < 2:
                        cross(source, tree, chunk, 0)
                    if plane == 3 and tree >= 2:
                        cross(source, tree, chunk, 1)
                    pass_on(source, tree, CHUNKS + chunk, ROOT_WAY[tree])

    @pl.when(worker)
    def _():
        leaf = [bit(LEAF[t]) == 1 for t in range(TREES)]
        first = [bit(FIRST[d]) == 1 for d in range(4)]
        starts = [(number(BEHIND_BITS[d]) * LEVEL) // 10 for d in range(4)]
        lengths = [bit(OUT[d]) * PLACES for d in range(4)]

        def body(step, carry):
            for way in range(4):
                place = step - starts[way]

                @pl.when((place >= 0) & (place < lengths[way]))
                def _(way=way, place=place):
                    tree = out_tree[way]

                    @pl.when(first[way])
                    def _():
                        take(tree, place)

                    pass_on(stream.at[places(tree, place), :], tree, place, way)

            return carry

        lax.fori_loop(0, PLACES + LONGEST, body, 0)

        for tree in range(TREES):

            @pl.when(leaf[tree])
            def _(tree=tree):
                def rest(place, carry):
                    take(tree, place)
                    return carry

                lax.fori_loop(0, PLACES, rest, 0)

        load_mine.wait()
        load_table.wait()

        @pl.when(first_plane)
        def _():
            load_above.wait()

        @pl.when(r != 0)
        def _():
            send_above(0).wait_recv()

        place = lax.broadcasted_iota(jnp.int32, (PIV, COLS), 0)
        across = lax.broadcasted_iota(jnp.int32, (PIV, COLS), 1)
        keep = jnp.where(
            place < B,
            jnp.where(across < B, patterns[2, 2 * c], patterns[2, 2 * c + 1]),
            jnp.where(across < B, patterns[3, 2 * c], patterns[3, 2 * c + 1]),
        )
        right = split(jnp.where(keep != 0, above[...], 0.0))
        solve = jnp.concatenate(
            [
                stream[pl.ds(pl.multiple_of(tree * SPAN + ahead * CROWS, CROWS), IQUARTER), :]
                for tree in range(TREES)
            ],
            axis=0,
        )
        solved = split(stacked_dot(split(solve), right))
        stack = jnp.concatenate([solved[0], solved[1], solved[0]], axis=0)

        def block_row(index):
            chunk = index * B // CROWS % CHUNKS
            start = index * B // QUARTER * SPAN + chunk * CROWS
            if chunk >= AHEAD:
                start = start + jnp.where(first_plane, ICHUNKS * CROWS, 0)
            block = stream[pl.ds(pl.multiple_of(start, CROWS), B), :]
            i = r * (ROWS // B) + index
            keep = jnp.where(across[:B] < B, patterns[0, i], patterns[1, i])
            return split(jnp.where(keep != 0, block, 0.0))

        def exchange(tile):
            rows = pl.ds(tile * TILE, TILE)
            return pltpu.make_async_remote_copy(
                mine.at[rows, :], peer.at[rows, :], peer_send, peer_recv.at[tile],
                device_id=other, device_id_type=MESH,
            )

        def store_out(tile):
            rows = pl.ds(tile * TILE, TILE)
            return pltpu.make_async_copy(total.at[rows, :], out.at[rows, :], out_sem)

        for tile in range(TILES + LATER):
            if tile < TILES:
                rows = slice(tile * TILE, (tile + 1) * TILE)
                parts = [block_row(tile * (TILE // B) + b) for b in range(TILE // B)]
                high = jnp.concatenate([part[0] for part in parts], axis=0)
                low = jnp.concatenate([part[1] for part in parts], axis=0)
                left = jnp.concatenate([high, high, low], axis=1)
                update = mine[rows, :] - jnp.dot(left, stack, preferred_element_type=jnp.float32)
                if tile * TILE < PIV:
                    update = jnp.where(r != 0, update, 0.0)
                mine[rows, :] = update
                exchange(tile).start()
            if tile >= LATER:
                done = tile - LATER
                rows = slice(done * TILE, (done + 1) * TILE)
                exchange(done).wait_recv()
                total[rows, :] = mine[rows, :] + peer[rows, :]
                store_out(done).start()

        pltpu.make_async_copy(total, out, out_sem).wait()
        pltpu.make_async_copy(mine, mine, peer_send).wait()

        @pl.when(first_plane)
        def _():
            for slot in range(3):
                send_above(slot).wait_send()

    @pl.when(root)
    def _():
        total[...] = jnp.zeros_like(total)
        clear = pltpu.make_async_copy(total, out, out_sem)
        clear.start()
        clear.wait()

    def sent(rows, semaphore):
        pltpu.make_async_copy(stream.at[0:rows, :], stream.at[0:rows, :], semaphore).wait()

    for way in range(4):

        @pl.when(bit(OUT[way]) == 1)
        def _(way=way):
            sent(SPAN, send_sem.at[way])

    for tree in range(TREES):
        for way, crossed in enumerate((plus[tree], minus[tree])):

            @pl.when(crossed)
            def _(tree=tree, way=way):
                sent(IQUARTER, cross_sem.at[tree, way])


def shards(front_matrix, row_pattern, col_pattern):
    f32, i32 = jnp.float32, jnp.int32
    dma = pltpu.SemaphoreType.DMA
    return pl.pallas_call(
        kernel,
        out_shape=jax.ShapeDtypeStruct((ROWS, COLS), f32),
        in_specs=[pl.BlockSpec(memory_space=pltpu.HBM)] * 2,
        out_specs=pl.BlockSpec(memory_space=pl.ANY),
        scratch_shapes=[
            pltpu.VMEM((TREES * SPAN, COLS), f32),
            pltpu.VMEM((ROWS, COLS), f32),
            pltpu.VMEM((PIV, COLS), f32),
            pltpu.VMEM((PIV, PIV), f32),
            pltpu.VMEM((ROWS, COLS), f32),
            pltpu.VMEM((ROWS, COLS), f32),
            pltpu.SMEM((4, 64), i32),
            dma((TREES, PLACES)),
            dma((4,)),
            dma((TREES, 2)),
            dma(()),
            dma((3,)),
            dma((TILES,)),
            dma(()),
            dma(()),
            dma((4,)),
        ],
        compiler_params=pltpu.CompilerParams(
            collective_id=0, has_side_effects=True, vmem_limit_bytes=50 * 1024 * 1024
        ),
        cost_estimate=pl.CostEstimate(
            flops=2 * ROWS * COLS * PIV, bytes_accessed=6 * ROWS * COLS * 4, transcendentals=0
        ),
        name="panel_update",
    )(front_matrix, jnp.concatenate([row_pattern, col_pattern]))


def solution(mesh):
    in_specs = (P("grp", "row", "col"), P(), P())
    out_specs = P("row", "col")
    return jax.shard_map(shards, mesh=mesh, in_specs=in_specs, out_specs=out_specs, check_vma=False)
```
